32 devices in a mesh: dp: 4 (over z), proto: 8 (over y, x, core).
Axes of the slice: x: 2, y: 2, z: 4, core: 2. Of those that a mesh axis runs over, the one named last changes fastest.
Arguments:
- teacher_rows: bfloat16 [1024, 256], P(('dp', 'proto')), may hold values from -48 to 48
- student_rows: bfloat16 [1024, 256], P(('dp', 'proto')), may hold values from -48 to 48
- teacher_protos: bfloat16 [65536, 256], P('proto'), may hold values from -48 to 48
- student_protos: bfloat16 [65536, 256], P('proto'), may hold values from -48 to 48
Outputs:
- row_grads: float32 [1024, 256], P(('dp', 'proto'))
- proto_grads: float32 [65536, 256], P('proto')
The draws below stay inside these ranges and needn't reach their ends.
All inputs are finite; a program needn't handle non-finite values.
Results may differ from the reference program's by a relative error of at most 0.0034.
Values may be sent and summed in bfloat16 or wider, within the bound.
A program may use at most 128 MiB of HBM per device.

```python
import jax
import jax.numpy as jnp
from jax import lax

D = 256
PROTO_DEV = 8192
ITERS = 3
PROTOS = 65536
ROWS = 1024


group_count = 64


def shared_parts(key):
    means = jnp.clip(jax.random.normal(jax.random.fold_in(key, 101), (group_count, D), jnp.float32), -4.0, 4.0)
    picks = jax.random.randint(jax.random.fold_in(key, 102), (ROWS,), 0, group_count)
    shifts = jax.random.randint(jax.random.fold_in(key, 103), (ROWS,), 0, group_count.bit_length())
    order = jax.random.permutation(jax.random.fold_in(key, 104), group_count)
    row_group = order[jnp.right_shift(picks, shifts)]
    proto_group = jax.random.randint(jax.random.fold_in(key, 105), (PROTOS,), 0, group_count)
    return (means, row_group, proto_group)


def row_base(key):
    means, row_group, proto_group = shared_parts(key)
    spread = jax.random.uniform(jax.random.fold_in(key, 106), (ROWS, 1), jnp.float32, 0.8, 2.0)
    noise = jnp.clip(jax.random.normal(jax.random.fold_in(key, 107), (ROWS, D), jnp.float32), -4.0, 4.0)
    return means[row_group] + spread * noise


def proto_base(key):
    means, row_group, proto_group = shared_parts(key)
    spread = jax.random.uniform(jax.random.fold_in(key, 108), (PROTOS, 1), jnp.float32, 0.5, 1.0)
    noise = jnp.clip(jax.random.normal(jax.random.fold_in(key, 109), (PROTOS, D), jnp.float32), -4.0, 4.0)
    return means[proto_group] + spread * noise


def draw_teacher_rows(key, part):
    base = row_base(key)
    key = jax.random.fold_in(key, 1)
    own = jnp.clip(jax.random.normal(key, (ROWS, D), jnp.float32), -4.0, 4.0)
    values = base + 0.5 * own
    return jnp.clip(values, -48.0, 48.0).astype(jnp.bfloat16)


def draw_student_rows(key, part):
    base = row_base(key)
    key = jax.random.fold_in(key, 2)
    own = jnp.clip(jax.random.normal(key, (ROWS, D), jnp.float32), -4.0, 4.0)
    values = base + 0.5 * own
    return jnp.clip(values, -48.0, 48.0).astype(jnp.bfloat16)


def draw_teacher_protos(key, part):
    base = proto_base(key)
    key = jax.random.fold_in(key, 3)
    own = jnp.clip(jax.random.normal(key, (PROTOS, D), jnp.float32), -4.0, 4.0)
    values = base + 0.1 * own
    return jnp.clip(values, -48.0, 48.0).astype(jnp.bfloat16)


def draw_student_protos(key, part):
    base = proto_base(key)
    key = jax.random.fold_in(key, 4)
    own = jnp.clip(jax.random.normal(key, (PROTOS, D), jnp.float32), -4.0, 4.0)
    values = base + 0.35 * own
    return jnp.clip(values, -48.0, 48.0).astype(jnp.bfloat16)


def setup_inputs(seed: int = 0) -> dict:
    splits = jax.random.split(jax.random.key(seed), 5)
    return {
        "teacher_rows": draw_teacher_rows(jax.random.fold_in(splits[4], 71), 0),
        "student_rows": draw_student_rows(jax.random.fold_in(splits[4], 71), 0),
        "teacher_protos": draw_teacher_protos(jax.random.fold_in(splits[4], 71), 0),
        "student_protos": draw_student_protos(jax.random.fold_in(splits[4], 71), 0),
    }


teacher_temp = 0.04
student_temp = 0.1
norm_eps = 1e-06

def unit_rows(values):
    vf = values.astype(jnp.float32)
    length = jnp.sqrt(lax.optimization_barrier(jnp.sum(vf * vf, axis=-1, keepdims=True)) + norm_eps)
    return (vf / length, length)

def rounded(values):
    held = lax.optimization_barrier(values.astype(jnp.bfloat16))
    return held.astype(jnp.float32)

def reference(teacher_rows, student_rows, teacher_protos, student_protos):
    rows = teacher_rows.shape[0]
    protos = teacher_protos.shape[0]
    blocks = protos // PROTO_DEV
    t_unit = rounded(unit_rows(teacher_rows)[0])
    s_unit = rounded(unit_rows(student_rows)[0])
    wt_unit = rounded(unit_rows(teacher_protos)[0]).reshape(blocks, PROTO_DEV, D)
    ws_full, ws_length = unit_rows(student_protos)
    ws_unit = rounded(ws_full).reshape(blocks, PROTO_DEV, D)

    def teach_exp(wblock):
        return jnp.exp(jnp.dot(t_unit, wblock.T) / teacher_temp)
    row_weight = jnp.ones((rows,), jnp.float32)
    col_blocks = None
    for step in range(ITERS):

        def sweep(acc, wblock, row_weight=row_weight):
            expo = teach_exp(wblock)
            col = 1.0 / (protos * jnp.dot(row_weight, expo, precision=lax.Precision.HIGHEST))
            return (acc + jnp.dot(expo, col, precision=lax.Precision.HIGHEST), col)
        acc, col_blocks = lax.scan(sweep, jnp.zeros((rows,), jnp.float32), wt_unit)
        row_weight = 1.0 / (rows * acc)

    def student_sum(acc, wblock):
        return (acc + lax.optimization_barrier(jnp.sum(jnp.exp(jnp.dot(s_unit, wblock.T) / student_temp), axis=1)), None)
    total, unused = lax.scan(student_sum, jnp.zeros((rows,), jnp.float32), ws_unit)

    def backward(acc, items):
        wtb, wsb, col = items
        targets = rows * teach_exp(wtb) * row_weight[:, None] * col[None, :]
        probs = jnp.exp(jnp.dot(s_unit, wsb.T) / student_temp) / total[:, None]
        grad_z = rounded((probs - targets) / student_temp)
        return (acc + jnp.dot(grad_z, wsb), jnp.dot(grad_z.T, s_unit))
    g_rows, g_blocks = lax.scan(backward, jnp.zeros((rows, D), jnp.float32), (wt_unit, ws_unit, col_blocks))
    g_protos = g_blocks.reshape(protos, D)
    s_full, s_length = unit_rows(student_rows)
    row_grads = (g_rows - lax.optimization_barrier(jnp.sum(g_rows * s_full, axis=1, keepdims=True)) * s_full) / s_length
    proto_grads = protos / rows * (g_protos - lax.optimization_barrier(jnp.sum(g_protos * ws_full, axis=1, keepdims=True)) * ws_full) / ws_length
    return (row_grads, proto_grads)
```

```python
import functools
import math

import jax
import jax.numpy as jnp
from jax import lax
from jax.experimental import pallas as pl
from jax.experimental.pallas import tpu as pltpu
from jax.sharding import PartitionSpec as P

ITERS = 3
LANES = 128

teacher_temp = 0.04
student_temp = 0.1
norm_eps = 1e-06
LOG2E = math.log2(math.e)
VMEM_BYTES = 56 * 1024 * 1024

MESH = pl.DeviceIdType.MESH
f32 = jnp.float32
bf16 = jnp.bfloat16


def inv_norm(vf):
    return lax.rsqrt(jnp.sum(vf * vf, axis=-1, keepdims=True) + norm_eps)


def unit_bf16(values):
    vf = values.astype(f32)
    return (vf * inv_norm(vf)).astype(bf16)


def dot_nn(a, b):
    return jnp.dot(a, b, preferred_element_type=f32)


def fold8(x):
    return jnp.sum(x.reshape(x.shape[0] // 8, 8, x.shape[1]), axis=0)


def greet(n_dp, n_proto):
    me_d, me_p = lax.axis_index("dp"), lax.axis_index("proto")
    barrier = pltpu.get_barrier_semaphore()
    for k in range(1, n_dp):
        pl.semaphore_signal(barrier, inc=1, device_id={"dp": lax.rem(me_d + k, n_dp)}, device_id_type=MESH)
    for k in range(1, n_proto):
        pl.semaphore_signal(barrier, inc=1, device_id={"proto": lax.rem(me_p + k, n_proto)}, device_id_type=MESH)
    return barrier


def sinkhorn_kernel(
    n_dp, n_proto, n_protos, tile, small,
    tT_ref, sT_ref, wt_hbm, ws_hbm, out_ref,
    e_ref, wt_ref, ws_ref, rxd, rxp, in_sem, sd, rd, sp, rp,
):
    n_rows = tT_ref.shape[1]
    own = wt_ref.shape[0]
    rb = n_rows // LANES
    me_d, me_p = lax.axis_index("dp"), lax.axis_index("proto")
    off = pl.multiple_of(me_d * own, own)
    in_t = pltpu.make_async_copy(wt_hbm.at[pl.ds(off, own)], wt_ref, in_sem.at[0])
    in_s = pltpu.make_async_copy(ws_hbm.at[pl.ds(off, own)], ws_ref, in_sem.at[1])
    in_t.start()
    in_s.start()
    barrier = greet(n_dp, n_proto)
    in_t.wait()

    zero = jnp.zeros((8, n_rows), f32)

    def first(i, acc):
        at = pl.ds(pl.multiple_of(i * tile, tile), tile)
        z = dot_nn(unit_bf16(wt_ref[at, :]), tT_ref[...])
        e = jnp.exp2(z * (LOG2E / teacher_temp))
        e_ref[at, :] = e
        col = 1.0 / (n_protos * jnp.sum(e, axis=1, keepdims=True))
        return acc + fold8(e * col)

    def student(i, acc):
        at = pl.ds(pl.multiple_of(i * tile, tile), tile)
        z = dot_nn(unit_bf16(ws_ref[at, :]), sT_ref[...])
        return acc + fold8(jnp.exp2(z * (LOG2E / student_temp)))

    def put(it, acc, part):
        row = jnp.sum(acc, axis=0, keepdims=True)
        for k in range(rb):
            rxd[it, me_d, part * rb + k : part * rb + k + 1, :] = row[:, k * LANES : (k + 1) * LANES]

    def take(tot, part):
        return jnp.concatenate([tot[part * rb + k : part * rb + k + 1, :] for k in range(rb)], axis=1)

    def sends(it, ref, me, n, axis, send, recv):
        copies = []
        for k in range(1, n):
            copies.append(
                pltpu.make_async_remote_copy(
                    src_ref=ref.at[it, me],
                    dst_ref=ref.at[it, me],
                    send_sem=send.at[it, k],
                    recv_sem=recv.at[it, k],
                    device_id={axis: lax.rem(me + k, n)},
                    device_id_type=MESH,
                )
            )
        for c in copies:
            c.start()
        return copies

    acc = lax.fori_loop(0, own // tile, first, zero)
    row_weight = jnp.ones((1, n_rows), f32)
    total = None
    acc_s = zero
    in_s.wait()
    for it in range(ITERS):
        prev = row_weight
        if it > 0:

            def again(i, acc, prev=prev):
                at = pl.ds(pl.multiple_of(i * small, small), small)
                e = e_ref[at, :]
                col = 1.0 / (n_protos * jnp.sum(e * prev, axis=1, keepdims=True))
                return acc + fold8(e * col)

            acc = lax.fori_loop(0, own // small, again, zero)
        put(it, acc, 0)
        put(it, acc_s, 1)
        if it == 0:
            pl.semaphore_wait(barrier, n_dp + n_proto - 2)
        copies = sends(it, rxd, me_d, n_dp, "dp", sd, rd)
        if it == 0:
            acc_s = lax.fori_loop(0, own // tile, student, zero)
        for c in copies:
            c.wait()
        part = rxd[it, 0]
        for k in range(1, n_dp):
            part = part + rxd[it, k]
        rxp[it, me_p] = part
        copies = sends(it, rxp, me_p, n_proto, "proto", sp, rp)
        for c in copies:
            c.wait()
        tot = rxp[it, 0]
        for k in range(1, n_proto):
            tot = tot + rxp[it, k]
        row_weight = 1.0 / (n_rows * take(tot, 0))
        total = take(tot, 1)
    out_ref[...] = jnp.zeros_like(out_ref)
    out_ref[0:1, :] = prev
    out_ref[1:2, :] = row_weight * (n_rows / student_temp)
    out_ref[2:3, :] = (1.0 / student_temp) / total


def sinkhorn(tT, sT, wt, ws, n_dp, n_proto):
    d, n_rows = tT.shape
    own = wt.shape[0] // n_dp
    rb = n_rows // LANES
    sems = pltpu.SemaphoreType.DMA
    vm = pl.BlockSpec(memory_space=pltpu.VMEM)
    anym = pl.BlockSpec(memory_space=pl.ANY)
    return pl.pallas_call(
        functools.partial(sinkhorn_kernel, n_dp, n_proto, wt.shape[0] * n_proto, 256, 32),
        out_shape=jax.ShapeDtypeStruct((8, n_rows), f32),
        in_specs=[vm, vm, anym, anym],
        out_specs=vm,
        scratch_shapes=[
            pltpu.VMEM((own, n_rows), f32),
            pltpu.VMEM((own, d), bf16),
            pltpu.VMEM((own, d), bf16),
            pltpu.VMEM((ITERS, n_dp, 2 * rb, LANES), f32),
            pltpu.VMEM((ITERS, n_proto, 2 * rb, LANES), f32),
            sems((2,)),
            sems((ITERS, n_dp)),
            sems((ITERS, n_dp)),
            sems((ITERS, n_proto)),
            sems((ITERS, n_proto)),
        ],
        compiler_params=pltpu.CompilerParams(collective_id=0, has_side_effects=True, vmem_limit_bytes=VMEM_BYTES),
        name="sinkhorn",
    )(tT, sT, wt, ws)


def backward_kernel(
    n_dp, n_protos, tT_ref, sT_ref, s_ref, rows_ref, wt_ref, ws_ref, out_ref, grow_ref, dz_ref
):
    n_rows = tT_ref.shape[1]
    mine = n_rows // n_dp
    a_prev, a_last, p_last = rows_ref[0:1, :], rows_ref[1:2, :], rows_ref[2:3, :]
    zt = dot_nn(unit_bf16(wt_ref[...]), tT_ref[...])
    wsf = ws_ref[...].astype(f32)
    ws_inv = inv_norm(wsf)
    ws_unit = wsf * ws_inv
    ws_half = ws_unit.astype(bf16)
    zs = dot_nn(ws_half, sT_ref[...])
    e = jnp.exp2(zt * (LOG2E / teacher_temp))
    col = 1.0 / (n_protos * jnp.sum(e * a_prev, axis=1, keepdims=True))
    probs = jnp.exp2(zs * (LOG2E / student_temp)) * p_last
    dz = (probs - (e * a_last) * col).astype(bf16)
    dz_ref[...] = dz
    g = dot_nn(dz, s_ref[...])
    factor = n_protos / n_rows
    proj = jnp.sum(g * ws_unit, axis=1, keepdims=True)
    out_ref[...] = (g - proj * ws_unit) * (factor * ws_inv)
    at = pl.multiple_of(lax.axis_index("dp") * mine, mine)
    part = lax.dot_general(
        dz_ref[:, pl.ds(at, mine)], ws_half, (((0,), (0,)), ((), ())), preferred_element_type=f32
    )

    @pl.when(pl.program_id(0) == 0)
    def _():
        grow_ref[...] = jnp.zeros_like(grow_ref)

    grow_ref[...] += part


def backward(tT, sT, s, rows, wt, ws, n_dp, n_proto, tile=256):
    d, n_rows = tT.shape
    n_own = wt.shape[0]
    const = lambda shape: pl.BlockSpec(shape, lambda i: (0, 0))
    tiled = pl.BlockSpec((tile, d), lambda i: (i, 0))
    mine = n_rows // n_dp
    return pl.pallas_call(
        functools.partial(backward_kernel, n_dp, n_own * n_proto),
        grid=(n_own // tile,),
        out_shape=(jax.ShapeDtypeStruct((n_own, d), f32), jax.ShapeDtypeStruct((mine, d), f32)),
        in_specs=[const((d, n_rows)), const((d, n_rows)), const((n_rows, d)), const((8, n_rows)), tiled, tiled],
        out_specs=(tiled, const((mine, d))),
        scratch_shapes=[pltpu.VMEM((tile, n_rows), bf16)],
        compiler_params=pltpu.CompilerParams(vmem_limit_bytes=VMEM_BYTES),
        name="backward",
    )(tT, sT, s, rows, wt, ws)


def scatter_kernel(n, g_ref, s_ref, out_ref, rx, send, recv):
    me = lax.axis_index("proto")
    own = out_ref.shape[0]
    barrier = pltpu.get_barrier_semaphore()
    for k in range(1, n):
        pl.semaphore_signal(barrier, inc=1, device_id={"proto": lax.rem(me + k, n)}, device_id_type=MESH)
    pl.semaphore_wait(barrier, n - 1)
    copies = []
    for k in range(1, n):
        to = lax.rem(me + k, n)
        copies.append(
            pltpu.make_async_remote_copy(
                src_ref=g_ref.at[pl.ds(pl.multiple_of(to * own, own), own)],
                dst_ref=rx.at[me],
                send_sem=send.at[k],
                recv_sem=recv.at[k],
                device_id={"proto": to},
                device_id_type=MESH,
            )
        )
    for c in copies:
        c.start()
    rx[me] = g_ref[pl.ds(pl.multiple_of(me * own, own), own), :]
    sf = s_ref[...].astype(f32)
    inv = inv_norm(sf)
    unit = sf * inv
    for c in copies:
        c.wait()
    g = rx[0]
    for k in range(1, n):
        g = g + rx[k]
    out_ref[...] = (g - jnp.sum(g * unit, axis=1, keepdims=True) * unit) * inv


def scatter_rows(grow, student_rows, n_proto):
    vm = pl.BlockSpec(memory_space=pltpu.VMEM)
    own, d = student_rows.shape
    return pl.pallas_call(
        functools.partial(scatter_kernel, n_proto),
        out_shape=jax.ShapeDtypeStruct((own, d), f32),
        in_specs=[vm, vm],
        out_specs=vm,
        scratch_shapes=[
            pltpu.VMEM((n_proto, own, d), f32),
            pltpu.SemaphoreType.DMA((n_proto,)),
            pltpu.SemaphoreType.DMA((n_proto,)),
        ],
        compiler_params=pltpu.CompilerParams(collective_id=1, has_side_effects=True),
        name="scatter_rows",
    )(grow, student_rows)


def body(teacher_rows, student_rows, teacher_protos, student_protos):
    n_dp, n_proto = lax.axis_size("dp"), lax.axis_size("proto")
    d = teacher_rows.shape[1]
    both = jnp.concatenate([unit_bf16(teacher_rows), unit_bf16(student_rows)], axis=1)
    both = lax.all_gather(both, ("dp", "proto"), axis=0, tiled=True)
    s_unit = both[:, d:]
    tT, sT = both[:, :d].T, s_unit.T
    rows = sinkhorn(tT, sT, teacher_protos, student_protos, n_dp, n_proto)
    proto_grads, grow = backward(tT, sT, s_unit, rows, teacher_protos, student_protos, n_dp, n_proto)
    row_grads = scatter_rows(grow, student_rows, n_proto)
    return (row_grads, proto_grads)


def solution(mesh):
    rows = P(("dp", "proto"), None)
    protos = P("proto", None)
    return jax.shard_map(
        body,
        mesh=mesh,
        in_specs=(rows, rows, protos, protos),
        out_specs=(rows, protos),
        check_vma=False,
    )
```

```python
import functools
import math

import jax
import jax.numpy as jnp
from jax import lax
from jax.experimental import pallas as pl
from jax.experimental.pallas import tpu as pltpu
from jax.sharding import PartitionSpec as P

ITERS = 3
LANES = 128

teacher_temp = 0.04
student_temp = 0.1
norm_eps = 1e-06
LOG2E = math.log2(math.e)
VMEM_BYTES = 56 * 1024 * 1024

MESH = pl.DeviceIdType.MESH
f32 = jnp.float32
bf16 = jnp.bfloat16


def inv_norm(vf):
    return lax.rsqrt(jnp.sum(vf * vf, axis=-1, keepdims=True) + norm_eps)


def unit_bf16(values):
    vf = values.astype(f32)
    return (vf * inv_norm(vf)).astype(bf16)


def dot_nn(a, b):
    return jnp.dot(a, b, preferred_element_type=f32)


def fold8(x):
    return jnp.sum(x.reshape(x.shape[0] // 8, 8, x.shape[1]), axis=0)


def greet(n_dp, n_proto):
    me_d, me_p = lax.axis_index("dp"), lax.axis_index("proto")
    barrier = pltpu.get_barrier_semaphore()
    for k in range(1, n_dp):
        pl.semaphore_signal(barrier, inc=1, device_id={"dp": lax.rem(me_d + k, n_dp)}, device_id_type=MESH)
    for k in range(1, n_proto):
        pl.semaphore_signal(barrier, inc=1, device_id={"proto": lax.rem(me_p + k, n_proto)}, device_id_type=MESH)
    return barrier


def sinkhorn_kernel(
    n_dp, n_proto, n_protos, tile, small, unroll,
    t_ref, s_ref, wt_hbm, ws_hbm, out_ref, tT_ref, sT_ref, su_ref,
    e_ref, wt_ref, ws_ref, gt, gs, rxd, rxp, in_sem, sz, rz, sx, rx, sc, rc, sd, rd, sp, rp,
):
    n_rows = tT_ref.shape[1]
    own = wt_ref.shape[0]
    rb = n_rows // LANES
    nq = n_proto // 2
    me_d, me_p = lax.axis_index("dp"), lax.axis_index("proto")
    q, c = lax.div(me_p, 2), lax.rem(me_p, 2)
    off = pl.multiple_of(me_d * own, own)
    in_t = pltpu.make_async_copy(wt_hbm.at[pl.ds(off, own)], wt_ref, in_sem.at[0])
    in_s = pltpu.make_async_copy(ws_hbm.at[pl.ds(off, own)], ws_ref, in_sem.at[1])
    in_t.start()
    in_s.start()
    barrier = greet(n_dp, n_proto)
    gt[me_d, me_p] = unit_bf16(t_ref[...])
    gs[me_d, me_p] = unit_bf16(s_ref[...])
    pl.semaphore_wait(barrier, n_dp + n_proto - 2)

    def remote(ref, send, recv, to):
        return pltpu.make_async_remote_copy(
            src_ref=ref, dst_ref=ref, send_sem=send, recv_sem=recv, device_id=to, device_id_type=MESH
        )

    def along_dp(w, buf):
        return [
            remote(buf.at[me_d, me_p], sz.at[w, k], rz.at[w, k], {"dp": lax.rem(me_d + k, n_dp)})
            for k in range(1, n_dp)
        ]

    def in_plane(w, buf):
        return [
            remote(buf.at[:, me_p], sx.at[w, k], rx.at[w, k], {"proto": 2 * lax.rem(q + k, nq) + c})
            for k in range(1, nq)
        ]

    def to_core(w, buf):
        return [
            remote(buf.at[:, 2 * lax.rem(q + nq - k, nq) + c], sc.at[w, k], rc.at[w, k], {"proto": me_p + 1 - 2 * c})
            for k in range(nq)
        ]

    bufs = (gt, gs)
    dps = [along_dp(w, bufs[w]) for w in range(2)]
    planes = [in_plane(w, bufs[w]) for w in range(2)]
    cores = [to_core(w, bufs[w]) for w in range(2)]
    for w in range(2):
        for copy in dps[w]:
            copy.start()

    def spread(w):
        for copy in dps[w]:
            copy.wait_recv()
        for copy in planes[w]:
            copy.start()
        cores[w][0].start()

    def hand_on(w):
        for k in range(1, nq):
            planes[w][k - 1].wait_recv()
            cores[w][k].start()

    def arrived(w):
        for copy in cores[w]:
            copy.wait_recv()

    spread(0)
    in_t.wait()
    wt_ref[...] = unit_bf16(wt_ref[...])
    spread(1)
    hand_on(0)
    in_s.wait()
    ws_ref[...] = unit_bf16(ws_ref[...])
    arrived(0)
    tT_ref[...] = gt[...].reshape(n_rows, gt.shape[3]).T

    zero = jnp.zeros((8, n_rows), f32)

    def first(i, acc):
        at = pl.ds(pl.multiple_of(i * tile, tile), tile)
        z = dot_nn(wt_ref[at, :], tT_ref[...])
        e = jnp.exp2(z * (LOG2E / teacher_temp))
        e_ref[at, :] = e
        col = 1.0 / (n_protos * jnp.sum(e, axis=1, keepdims=True))
        return acc + fold8(e * col)

    def student(i, acc):
        at = pl.ds(pl.multiple_of(i * tile, tile), tile)
        z = dot_nn(ws_ref[at, :], sT_ref[...])
        return acc + fold8(jnp.exp2(z * (LOG2E / student_temp)))

    def put(it, acc, part):
        row = jnp.sum(acc, axis=0, keepdims=True)
        for k in range(rb):
            rxd[it, me_d, part * rb + k : part * rb + k + 1, :] = row[:, k * LANES : (k + 1) * LANES]

    def take(tot, part):
        return jnp.concatenate([tot[part * rb + k : part * rb + k + 1, :] for k in range(rb)], axis=1)

    def sends(it, ref, me, n, axis, send, recv, rows):
        copies = [
            remote(ref.at[it, me, pl.ds(0, rows)], send.at[it, k], recv.at[it, k], {axis: lax.rem(me + k, n)})
            for k in range(1, n)
        ]
        for copy in copies:
            copy.start()
        return copies

    def total_of(it, ref, n, rows):
        tot = ref[it, 0, 0:rows, :]
        for k in range(1, n):
            tot = tot + ref[it, k, 0:rows, :]
        return tot

    acc = lax.fori_loop(0, own // tile, first, zero)
    row_weight = jnp.ones((1, n_rows), f32)
    acc_s = zero
    half = own // tile // 2
    late = []
    for it in range(ITERS):
        prev = row_weight
        if it > 0:

            def again(i, acc, prev=prev):
                for j in range(unroll):
                    at = pl.ds(pl.multiple_of((i * unroll + j) * small, small), small)
                    e = e_ref[at, :]
                    col = 1.0 / (n_protos * jnp.sum(e * prev, axis=1, keepdims=True))
                    acc = acc + fold8(e * col)
                return acc

            acc = lax.fori_loop(0, own // (small * unroll), again, zero)
        last = it == ITERS - 1
        rows = 2 * rb if last else rb
        put(it, acc, 0)
        if last:
            put(it, acc_s, 1)
        copies = sends(it, rxd, me_d, n_dp, "dp", sd, rd, rows)
        late += copies
        if it == 0:
            hand_on(1)
        if it == 1:
            acc_s = lax.fori_loop(0, half, student, acc_s)
        for copy in copies:
            copy.wait_recv()
        rxp[it, me_p, 0:rows, :] = total_of(it, rxd, n_dp, rows)
        copies = sends(it, rxp, me_p, n_proto, "proto", sp, rp, rows)
        late += copies
        if it == 0:
            arrived(1)
            su_ref[...] = gs[...].reshape(n_rows, gs.shape[3])
            sT_ref[...] = su_ref[...].T
        if it == 1:
            acc_s = lax.fori_loop(half, own // tile, student, acc_s)
        for copy in copies:
            copy.wait_recv()
        tot = total_of(it, rxp, n_proto, rows)
        row_weight = 1.0 / (n_rows * take(tot, 0))
    total = take(tot, 1)
    out_ref[...] = jnp.zeros_like(out_ref)
    out_ref[0:1, :] = prev
    out_ref[1:2, :] = row_weight * (n_rows / student_temp)
    out_ref[2:3, :] = (1.0 / student_temp) / total
    for w in range(2):
        late += dps[w] + planes[w] + cores[w]
    for copy in late:
        copy.wait_send()


def sinkhorn(t, s, wt, ws, n_dp, n_proto, tile=512, small=32, unroll=8):
    mine, d = t.shape
    n_rows = mine * n_dp * n_proto
    own = wt.shape[0] // n_dp
    rb = n_rows // LANES
    nq = n_proto // 2
    sems = pltpu.SemaphoreType.DMA
    vm = pl.BlockSpec(memory_space=pltpu.VMEM)
    anym = pl.BlockSpec(memory_space=pl.ANY)
    return pl.pallas_call(
        functools.partial(sinkhorn_kernel, n_dp, n_proto, wt.shape[0] * n_proto, tile, small, unroll),
        out_shape=(
            jax.ShapeDtypeStruct((8, n_rows), f32),
            jax.ShapeDtypeStruct((d, n_rows), bf16),
            jax.ShapeDtypeStruct((d, n_rows), bf16),
            jax.ShapeDtypeStruct((n_rows, d), bf16),
        ),
        in_specs=[vm, vm, anym, anym],
        out_specs=(vm, vm, vm, vm),
        scratch_shapes=[
            pltpu.VMEM((own, n_rows), f32),
            pltpu.VMEM((own, d), bf16),
            pltpu.VMEM((own, d), bf16),
            pltpu.VMEM((n_dp, n_proto, mine, d), bf16),
            pltpu.VMEM((n_dp, n_proto, mine, d), bf16),
            pltpu.VMEM((ITERS, n_dp, 2 * rb, LANES), f32),
            pltpu.VMEM((ITERS, n_proto, 2 * rb, LANES), f32),
            sems((2,)),
            sems((2, n_dp)),
            sems((2, n_dp)),
            sems((2, nq)),
            sems((2, nq)),
            sems((2, nq)),
            sems((2, nq)),
            sems((ITERS, n_dp)),
            sems((ITERS, n_dp)),
            sems((ITERS, n_proto)),
            sems((ITERS, n_proto)),
        ],
        compiler_params=pltpu.CompilerParams(collective_id=0, has_side_effects=True, vmem_limit_bytes=VMEM_BYTES),
        name="sinkhorn",
    )(t, s, wt, ws)


def backward_kernel(
    n_dp, n_protos, sub, tT_ref, sT_ref, s_ref, rows_ref, wt_ref, ws_ref, out_ref, grow_ref, dz_ref, wsh_ref
):
    n_rows = tT_ref.shape[1]
    mine = n_rows // n_dp
    factor = n_protos / n_rows
    a_prev, a_last, p_last = rows_ref[0:1, :], rows_ref[1:2, :], rows_ref[2:3, :]
    for j in range(wt_ref.shape[0] // sub):
        at = slice(j * sub, (j + 1) * sub)
        zt = dot_nn(unit_bf16(wt_ref[at, :]), tT_ref[...])
        wsf = ws_ref[at, :].astype(f32)
        ws_inv = inv_norm(wsf)
        ws_unit = wsf * ws_inv
        ws_half = ws_unit.astype(bf16)
        wsh_ref[at, :] = ws_half
        zs = dot_nn(ws_half, sT_ref[...])
        e = jnp.exp2(zt * (LOG2E / teacher_temp))
        col = 1.0 / (n_protos * jnp.sum(e * a_prev, axis=1, keepdims=True))
        probs = jnp.exp2(zs * (LOG2E / student_temp)) * p_last
        dz = (probs - (e * a_last) * col).astype(bf16)
        dz_ref[at, :] = dz
        g = dot_nn(dz, s_ref[...])
        proj = jnp.sum(g * ws_unit, axis=1, keepdims=True)
        out_ref[at, :] = (g - proj * ws_unit) * (factor * ws_inv)
    own_rows = pl.ds(pl.multiple_of(lax.axis_index("dp") * mine, mine), mine)
    part = lax.dot_general(
        dz_ref[:, own_rows], wsh_ref[...], (((0,), (0,)), ((), ())), preferred_element_type=f32
    )

    @pl.when(pl.program_id(0) == 0)
    def _():
        grow_ref[...] = jnp.zeros_like(grow_ref)

    grow_ref[...] += part


def backward(tT, sT, s, rows, wt, ws, n_dp, n_proto, tile=None, sub=None):
    d, n_rows = tT.shape
    n_own = wt.shape[0]
    tile = tile or max(256, (1 << 20) // n_rows)
    sub = sub or 256
    const = lambda shape: pl.BlockSpec(shape, lambda i: (0, 0))
    tiled = pl.BlockSpec((tile, d), lambda i: (i, 0))
    mine = n_rows // n_dp
    return pl.pallas_call(
        functools.partial(backward_kernel, n_dp, n_own * n_proto, sub),
        grid=(n_own // tile,),
        out_shape=(jax.ShapeDtypeStruct((n_own, d), f32), jax.ShapeDtypeStruct((mine, d), f32)),
        in_specs=[const((d, n_rows)), const((d, n_rows)), const((n_rows, d)), const((8, n_rows)), tiled, tiled],
        out_specs=(tiled, const((mine, d))),
        scratch_shapes=[pltpu.VMEM((tile, n_rows), bf16), pltpu.VMEM((tile, d), bf16)],
        compiler_params=pltpu.CompilerParams(vmem_limit_bytes=VMEM_BYTES),
        name="backward",
    )(tT, sT, s, rows, wt, ws)


def scatter_kernel(n, g_ref, s_ref, out_ref, rx, send, recv):
    me = lax.axis_index("proto")
    own = out_ref.shape[0]
    barrier = pltpu.get_barrier_semaphore()
    for k in range(1, n):
        pl.semaphore_signal(barrier, inc=1, device_id={"proto": lax.rem(me + k, n)}, device_id_type=MESH)
    pl.semaphore_wait(barrier, n - 1)
    copies = []
    for k in range(1, n):
        to = lax.rem(me + k, n)
        copies.append(
            pltpu.make_async_remote_copy(
                src_ref=g_ref.at[pl.ds(pl.multiple_of(to * own, own), own)],
                dst_ref=rx.at[me],
                send_sem=send.at[k],
                recv_sem=recv.at[k],
                device_id={"proto": to},
                device_id_type=MESH,
            )
        )
    for c in copies:
        c.start()
    rx[me] = g_ref[pl.ds(pl.multiple_of(me * own, own), own), :]
    sf = s_ref[...].astype(f32)
    inv = inv_norm(sf)
    unit = sf * inv
    for c in copies:
        c.wait()
    g = rx[0]
    for k in range(1, n):
        g = g + rx[k]
    out_ref[...] = (g - jnp.sum(g * unit, axis=1, keepdims=True) * unit) * inv


def scatter_rows(grow, student_rows, n_proto):
    vm = pl.BlockSpec(memory_space=pltpu.VMEM)
    own, d = student_rows.shape
    return pl.pallas_call(
        functools.partial(scatter_kernel, n_proto),
        out_shape=jax.ShapeDtypeStruct((own, d), f32),
        in_specs=[vm, vm],
        out_specs=vm,
        scratch_shapes=[
            pltpu.VMEM((n_proto, own, d), f32),
            pltpu.SemaphoreType.DMA((n_proto,)),
            pltpu.SemaphoreType.DMA((n_proto,)),
        ],
        compiler_params=pltpu.CompilerParams(collective_id=1, has_side_effects=True),
        name="scatter_rows",
    )(grow, student_rows)


def body(teacher_rows, student_rows, teacher_protos, student_protos):
    n_dp, n_proto = lax.axis_size("dp"), lax.axis_size("proto")
    stats, tT, sT, s_unit = sinkhorn(teacher_rows, student_rows, teacher_protos, student_protos, n_dp, n_proto)
    proto_grads, grow = backward(tT, sT, s_unit, stats, teacher_protos, student_protos, n_dp, n_proto)
    row_grads = scatter_rows(grow, student_rows, n_proto)
    return (row_grads, proto_grads)


def solution(mesh):
    rows = P(("dp", "proto"), None)
    protos = P("proto", None)
    return jax.shard_map(
        body,
        mesh=mesh,
        in_specs=(rows, rows, protos, protos),
        out_specs=(rows, protos),
        check_vma=False,
    )
```

```python
import functools
import math

import jax
import jax.numpy as jnp
from jax import lax
from jax.experimental import pallas as pl
from jax.experimental.pallas import tpu as pltpu
from jax.sharding import PartitionSpec as P

ITERS = 3
LANES = 128

teacher_temp = 0.04
student_temp = 0.1
norm_eps = 1e-06
LOG2E = math.log2(math.e)
VMEM_BYTES = 56 * 1024 * 1024

MESH = pl.DeviceIdType.MESH
f32 = jnp.float32
bf16 = jnp.bfloat16


def inv_norm(vf):
    return lax.rsqrt(jnp.sum(vf * vf, axis=-1, keepdims=True) + norm_eps)


def unit_bf16(values):
    vf = values.astype(f32)
    return (vf * inv_norm(vf)).astype(bf16)


def dot_nn(a, b):
    return jnp.dot(a, b, preferred_element_type=f32)


def fold8(x):
    return jnp.sum(x.reshape(x.shape[0] // 8, 8, x.shape[1]), axis=0)


def greet(n_dp, n_proto):
    me_d, me_p = lax.axis_index("dp"), lax.axis_index("proto")
    barrier = pltpu.get_barrier_semaphore()
    for k in range(1, n_dp):
        pl.semaphore_signal(barrier, inc=1, device_id={"dp": lax.rem(me_d + k, n_dp)}, device_id_type=MESH)
    for k in range(1, n_proto):
        pl.semaphore_signal(barrier, inc=1, device_id={"proto": lax.rem(me_p + k, n_proto)}, device_id_type=MESH)
    return barrier


def sinkhorn_kernel(
    n_dp, n_proto, n_protos, tile, small, unroll,
    t_ref, s_ref, wt_hbm, ws_hbm, out_ref, tT_ref, sT_ref, su_ref,
    e_ref, wt_ref, ws_ref, gt, gs, rxd, rxp, in_sem, sz, rz, sx, rx, sc, rc, sd, rd, sp, rp,
):
    n_rows = tT_ref.shape[1]
    own = wt_ref.shape[0]
    rb = n_rows // LANES
    nq = n_proto // 2
    me_d, me_p = lax.axis_index("dp"), lax.axis_index("proto")
    q, c = lax.div(me_p, 2), lax.rem(me_p, 2)
    off = pl.multiple_of(me_d * own, own)
    in_t = pltpu.make_async_copy(wt_hbm.at[pl.ds(off, own)], wt_ref, in_sem.at[0])
    in_s = pltpu.make_async_copy(ws_hbm.at[pl.ds(off, own)], ws_ref, in_sem.at[1])
    in_t.start()
    in_s.start()
    barrier = greet(n_dp, n_proto)
    gt[me_d, me_p] = unit_bf16(t_ref[...])
    gs[me_d, me_p] = unit_bf16(s_ref[...])
    pl.semaphore_wait(barrier, n_dp + n_proto - 2)

    def remote(ref, send, recv, to):
        return pltpu.make_async_remote_copy(
            src_ref=ref, dst_ref=ref, send_sem=send, recv_sem=recv, device_id=to, device_id_type=MESH
        )

    def along_dp(w, buf):
        return [
            remote(buf.at[me_d, me_p], sz.at[w, k], rz.at[w, k], {"dp": lax.rem(me_d + k, n_dp)})
            for k in range(1, n_dp)
        ]

    def in_plane(w, buf):
        return [
            [
                remote(
                    buf.at[lax.rem(me_d + n_dp - d, n_dp), me_p],
                    sx.at[w, d, k], rx.at[w, d, k], {"proto": 2 * lax.rem(q + k, nq) + c},
                )
                for k in range(1, nq)
            ]
            for d in range(n_dp)
        ]

    def to_core(w, buf):
        return [
            [
                remote(
                    buf.at[lax.rem(me_d + n_dp - d, n_dp), 2 * lax.rem(q + nq - k, nq) + c],
                    sc.at[w, d, k], rc.at[w, d, k], {"proto": me_p + 1 - 2 * c},
                )
                for k in range(nq)
            ]
            for d in range(n_dp)
        ]

    bufs = (gt, gs)
    dps = [along_dp(w, bufs[w]) for w in range(2)]
    planes = [in_plane(w, bufs[w]) for w in range(2)]
    cores = [to_core(w, bufs[w]) for w in range(2)]
    for copy in dps[0]:
        copy.start()

    def spread(w, ds):
        for d in ds:
            if d:
                dps[w][d - 1].wait_recv()
            for copy in planes[w][d]:
                copy.start()
            cores[w][d][0].start()

    def hand_on(w):
        for d in range(n_dp):
            for k in range(1, nq):
                planes[w][d][k - 1].wait_recv()
                cores[w][d][k].start()

    def arrived(w):
        for row in cores[w]:
            for copy in row:
                copy.wait_recv()

    spread(0, [0])
    for copy in dps[1]:
        copy.start()
    spread(0, range(1, n_dp))
    in_t.wait()
    wt_ref[...] = unit_bf16(wt_ref[...])
    hand_on(0)
    spread(1, range(n_dp))
    in_s.wait()
    ws_ref[...] = unit_bf16(ws_ref[...])
    arrived(0)
    tT_ref[...] = gt[...].reshape(n_rows, gt.shape[3]).T

    zero = jnp.zeros((8, n_rows), f32)

    def first(i, acc):
        at = pl.ds(pl.multiple_of(i * tile, tile), tile)
        z = dot_nn(wt_ref[at, :], tT_ref[...])
        e = jnp.exp2(z * (LOG2E / teacher_temp))
        e_ref[at, :] = e
        col = 1.0 / (n_protos * jnp.sum(e, axis=1, keepdims=True))
        return acc + fold8(e * col)

    def student(i, acc):
        at = pl.ds(pl.multiple_of(i * tile, tile), tile)
        z = dot_nn(ws_ref[at, :], sT_ref[...])
        return acc + fold8(jnp.exp2(z * (LOG2E / student_temp)))

    def put(it, acc, part):
        row = jnp.sum(acc, axis=0, keepdims=True)
        for k in range(rb):
            rxd[it, me_d, part * rb + k : part * rb + k + 1, :] = row[:, k * LANES : (k + 1) * LANES]

    def take(tot, part):
        return jnp.concatenate([tot[part * rb + k : part * rb + k + 1, :] for k in range(rb)], axis=1)

    def sends(it, ref, me, n, axis, send, recv, rows):
        copies = [
            remote(ref.at[it, me, pl.ds(0, rows)], send.at[it, k], recv.at[it, k], {axis: lax.rem(me + k, n)})
            for k in range(1, n)
        ]
        for copy in copies:
            copy.start()
        return copies

    def total_of(it, ref, n, rows):
        tot = ref[it, 0, 0:rows, :]
        for k in range(1, n):
            tot = tot + ref[it, k, 0:rows, :]
        return tot

    acc = lax.fori_loop(0, own // tile, first, zero)
    row_weight = jnp.ones((1, n_rows), f32)
    acc_s = zero
    half = own // tile // 2
    late = []
    for it in range(ITERS):
        prev = row_weight
        if it > 0:

            def again(i, acc, prev=prev):
                for j in range(unroll):
                    at = pl.ds(pl.multiple_of((i * unroll + j) * small, small), small)
                    e = e_ref[at, :]
                    col = 1.0 / (n_protos * jnp.sum(e * prev, axis=1, keepdims=True))
                    acc = acc + fold8(e * col)
                return acc

            acc = lax.fori_loop(0, own // (small * unroll), again, zero)
        last = it == ITERS - 1
        rows = 2 * rb if last else rb
        put(it, acc, 0)
        if last:
            put(it, acc_s, 1)
        copies = sends(it, rxd, me_d, n_dp, "dp", sd, rd, rows)
        late += copies
        if it == 0:
            hand_on(1)
        if it == 1:
            acc_s = lax.fori_loop(0, half, student, acc_s)
        for copy in copies:
            copy.wait_recv()
        rxp[it, me_p, 0:rows, :] = total_of(it, rxd, n_dp, rows)
        copies = sends(it, rxp, me_p, n_proto, "proto", sp, rp, rows)
        late += copies
        if it == 0:
            arrived(1)
            su_ref[...] = gs[...].reshape(n_rows, gs.shape[3])
            sT_ref[...] = su_ref[...].T
        if it == 1:
            acc_s = lax.fori_loop(half, own // tile, student, acc_s)
        for copy in copies:
            copy.wait_recv()
        tot = total_of(it, rxp, n_proto, rows)
        row_weight = 1.0 / (n_rows * take(tot, 0))
    total = take(tot, 1)
    out_ref[...] = jnp.zeros_like(out_ref)
    out_ref[0:1, :] = prev
    out_ref[1:2, :] = row_weight * (n_rows / student_temp)
    out_ref[2:3, :] = (1.0 / student_temp) / total
    for w in range(2):
        late += dps[w] + sum(planes[w], []) + sum(cores[w], [])
    for copy in late:
        copy.wait_send()


def sinkhorn(t, s, wt, ws, n_dp, n_proto, tile=512, small=32, unroll=8):
    mine, d = t.shape
    n_rows = mine * n_dp * n_proto
    own = wt.shape[0] // n_dp
    rb = n_rows // LANES
    nq = n_proto // 2
    sems = pltpu.SemaphoreType.DMA
    vm = pl.BlockSpec(memory_space=pltpu.VMEM)
    anym = pl.BlockSpec(memory_space=pl.ANY)
    return pl.pallas_call(
        functools.partial(sinkhorn_kernel, n_dp, n_proto, wt.shape[0] * n_proto, tile, small, unroll),
        out_shape=(
            jax.ShapeDtypeStruct((8, n_rows), f32),
            jax.ShapeDtypeStruct((d, n_rows), bf16),
            jax.ShapeDtypeStruct((d, n_rows), bf16),
            jax.ShapeDtypeStruct((n_rows, d), bf16),
        ),
        in_specs=[vm, vm, anym, anym],
        out_specs=(vm, vm, vm, vm),
        scratch_shapes=[
            pltpu.VMEM((own, n_rows), f32),
            pltpu.VMEM((own, d), bf16),
            pltpu.VMEM((own, d), bf16),
            pltpu.VMEM((n_dp, n_proto, mine, d), bf16),
            pltpu.VMEM((n_dp, n_proto, mine, d), bf16),
            pltpu.VMEM((ITERS, n_dp, 2 * rb, LANES), f32),
            pltpu.VMEM((ITERS, n_proto, 2 * rb, LANES), f32),
            sems((2,)),
            sems((2, n_dp)),
            sems((2, n_dp)),
            sems((2, n_dp, nq)),
            sems((2, n_dp, nq)),
            sems((2, n_dp, nq)),
            sems((2, n_dp, nq)),
            sems((ITERS, n_dp)),
            sems((ITERS, n_dp)),
            sems((ITERS, n_proto)),
            sems((ITERS, n_proto)),
        ],
        compiler_params=pltpu.CompilerParams(collective_id=0, has_side_effects=True, vmem_limit_bytes=VMEM_BYTES),
        name="sinkhorn",
    )(t, s, wt, ws)


def backward_kernel(
    n_dp, n_protos, sub, tT_ref, sT_ref, s_ref, rows_ref, wt_ref, ws_ref, out_ref, grow_ref, dz_ref, wsh_ref
):
    n_rows = tT_ref.shape[1]
    mine = n_rows // n_dp
    factor = n_protos / n_rows
    a_prev, a_last, p_last = rows_ref[0:1, :], rows_ref[1:2, :], rows_ref[2:3, :]
    for j in range(wt_ref.shape[0] // sub):
        at = slice(j * sub, (j + 1) * sub)
        zt = dot_nn(unit_bf16(wt_ref[at, :]), tT_ref[...])
        wsf = ws_ref[at, :].astype(f32)
        ws_inv = inv_norm(wsf)
        ws_unit = wsf * ws_inv
        ws_half = ws_unit.astype(bf16)
        wsh_ref[at, :] = ws_half
        zs = dot_nn(ws_half, sT_ref[...])
        e = jnp.exp2(zt * (LOG2E / teacher_temp))
        col = 1.0 / (n_protos * jnp.sum(e * a_prev, axis=1, keepdims=True))
        probs = jnp.exp2(zs * (LOG2E / student_temp)) * p_last
        dz = (probs - (e * a_last) * col).astype(bf16)
        dz_ref[at, :] = dz
        g = dot_nn(dz, s_ref[...])
        proj = jnp.sum(g * ws_unit, axis=1, keepdims=True)
        out_ref[at, :] = (g - proj * ws_unit) * (factor * ws_inv)
    own_rows = pl.ds(pl.multiple_of(lax.axis_index("dp") * mine, mine), mine)
    part = lax.dot_general(
        dz_ref[:, own_rows], wsh_ref[...], (((0,), (0,)), ((), ())), preferred_element_type=f32
    )

    @pl.when(pl.program_id(0) == 0)
    def _():
        grow_ref[...] = jnp.zeros_like(grow_ref)

    grow_ref[...] += part


def backward(tT, sT, s, rows, wt, ws, n_dp, n_proto, tile=None, sub=None):
    d, n_rows = tT.shape
    n_own = wt.shape[0]
    tile = tile or max(256, (1 << 20) // n_rows)
    sub = sub or 256
    const = lambda shape: pl.BlockSpec(shape, lambda i: (0, 0))
    tiled = pl.BlockSpec((tile, d), lambda i: (i, 0))
    mine = n_rows // n_dp
    return pl.pallas_call(
        functools.partial(backward_kernel, n_dp, n_own * n_proto, sub),
        grid=(n_own // tile,),
        out_shape=(jax.ShapeDtypeStruct((n_own, d), f32), jax.ShapeDtypeStruct((mine, d), f32)),
        in_specs=[const((d, n_rows)), const((d, n_rows)), const((n_rows, d)), const((8, n_rows)), tiled, tiled],
        out_specs=(tiled, const((mine, d))),
        scratch_shapes=[pltpu.VMEM((tile, n_rows), bf16), pltpu.VMEM((tile, d), bf16)],
        compiler_params=pltpu.CompilerParams(vmem_limit_bytes=VMEM_BYTES),
        name="backward",
    )(tT, sT, s, rows, wt, ws)


def scatter_kernel(n, g_ref, s_ref, out_ref, rx, send, recv):
    me = lax.axis_index("proto")
    own = out_ref.shape[0]
    barrier = pltpu.get_barrier_semaphore()
    for k in range(1, n):
        pl.semaphore_signal(barrier, inc=1, device_id={"proto": lax.rem(me + k, n)}, device_id_type=MESH)
    pl.semaphore_wait(barrier, n - 1)
    copies = []
    for k in range(1, n):
        to = lax.rem(me + k, n)
        copies.append(
            pltpu.make_async_remote_copy(
                src_ref=g_ref.at[pl.ds(pl.multiple_of(to * own, own), own)],
                dst_ref=rx.at[me],
                send_sem=send.at[k],
                recv_sem=recv.at[k],
                device_id={"proto": to},
                device_id_type=MESH,
            )
        )
    for c in copies:
        c.start()
    rx[me] = g_ref[pl.ds(pl.multiple_of(me * own, own), own), :]
    sf = s_ref[...].astype(f32)
    inv = inv_norm(sf)
    unit = sf * inv
    for c in copies:
        c.wait()
    g = rx[0]
    for k in range(1, n):
        g = g + rx[k]
    out_ref[...] = (g - jnp.sum(g * unit, axis=1, keepdims=True) * unit) * inv


def scatter_rows(grow, student_rows, n_proto):
    vm = pl.BlockSpec(memory_space=pltpu.VMEM)
    own, d = student_rows.shape
    return pl.pallas_call(
        functools.partial(scatter_kernel, n_proto),
        out_shape=jax.ShapeDtypeStruct((own, d), f32),
        in_specs=[vm, vm],
        out_specs=vm,
        scratch_shapes=[
            pltpu.VMEM((n_proto, own, d), f32),
            pltpu.SemaphoreType.DMA((n_proto,)),
            pltpu.SemaphoreType.DMA((n_proto,)),
        ],
        compiler_params=pltpu.CompilerParams(collective_id=1, has_side_effects=True),
        name="scatter_rows",
    )(grow, student_rows)


def body(teacher_rows, student_rows, teacher_protos, student_protos):
    n_dp, n_proto = lax.axis_size("dp"), lax.axis_size("proto")
    stats, tT, sT, s_unit = sinkhorn(teacher_rows, student_rows, teacher_protos, student_protos, n_dp, n_proto)
    proto_grads, grow = backward(tT, sT, s_unit, stats, teacher_protos, student_protos, n_dp, n_proto)
    row_grads = scatter_rows(grow, student_rows, n_proto)
    return (row_grads, proto_grads)


def solution(mesh):
    rows = P(("dp", "proto"), None)
    protos = P("proto", None)
    return jax.shard_map(
        body,
        mesh=mesh,
        in_specs=(rows, rows, protos, protos),
        out_specs=(rows, protos),
        check_vma=False,
    )
```
